32 devices in a mesh: replica: 2 (over x), req: 8 (over z, y), tp: 2 (over core).
Axes of the slice: x: 2, y: 2, z: 4, core: 2. Of those that a mesh axis runs over, the one named last changes fastest.
Arguments:
- normed_hidden_rows: bfloat16 [2048, 4096], P(('replica', 'req')), parts along dimension 0, may hold values from -30 to 30
- base_query_rows: bfloat16 [2048, 2048], P(('replica', 'req'), 'tp'), parts along dimension 0, may hold values from -20 to 20
- incoming_key: bfloat16 [2048, 2048], P(('replica', 'req'), 'tp'), parts along dimension 0, may hold values from -8 to 8
- base_value_rows: bfloat16 [2048, 2048], P(('replica', 'req'), 'tp'), parts along dimension 0, may hold values from -3 to 3
- stored_keys: bfloat16 [2048, 16, 2048], P(('replica', 'req'), None, 'tp'), parts along dimension 0, may hold values from -20 to 20
- stored_values: bfloat16 [2048, 16, 2048], P(('replica', 'req'), None, 'tp'), parts along dimension 0, may hold values from -3 to 3
- cache_fill_length: int32 [2048], P(('replica', 'req')), parts along dimension 0, may hold values from 2 to 16, as said below
- adapter_of_row: int32 [2048], P(('replica', 'req')), parts along dimension 0, may hold values from 0 to 127, as said below
- adapter_pool_row: int32 [256], P('replica'), parts along dimension 0, may hold values from 0 to 127, as said below
- output_projection_weight: bfloat16 [2048, 4096], P('tp'), may hold values from -0.125 to 0.125
- output_block_scales: float32 [16, 32], P('tp'), may hold values from 0.5 to 2
- query_value_down_maps: bfloat16 [128, 32, 4096], P('req'), may hold values from -0.09375 to 0.09375
- query_value_up_maps: bfloat16 [128, 32, 2048], P('req', None, 'tp'), may hold values from -1.5 to 1.5
- output_down_maps: bfloat16 [128, 16, 2048], P('req', None, 'tp'), may hold values from -0.125 to 0.125
- output_up_maps: bfloat16 [128, 16, 4096], P('req', None, 'tp'), may hold values from -1.5 to 1.5
Outputs:
- layer_out: bfloat16 [2048, 4096], P(('replica', 'req'), 'tp'), parts along dimension 0
The draws below stay inside these ranges and needn't reach their ends.
There are 2 independent parts, one for each index of `replica`. The reference program is written for one: setup_inputs(seed, part) draws one part's arguments, and reference() takes and returns one part's arrays. A program takes and returns all parts, laid end to end along the dimension named above; an argument that names none is the same for every part. Nothing has to cross between parts.
Inputs may be any that keep to these rules, and one draw needn't show every extreme that they name: A permutation: adapter a is stored at row adapter_pool_row[a] of every adapter array. `adapter_of_row`: the rows of one device name adapters stored on one request shard (adapter_pool_row[id] // 16) at most 32 times; on every device some shard is named exactly 32 times. `cache_fill_length`: on every device some row has all 16 positions filled.
All inputs are finite; a program needn't handle non-finite values.
Results may differ from the reference program's by a relative error of at most 0.015.
Values may be sent and summed in bfloat16 or wider, within the bound.
A program may use at most 128 MiB of HBM per device.

```python
import math
import jax
import jax.numpy as jnp
from jax import lax

MODEL_WIDTH = 4096
HEAD_DIM = 128
HEADS = 16
ADAPTER_RANK = 16
BLOCK = 128
ROWS_DEV = 128
CACHE = 16
ADAPT_DEV = 16
CAP = 32
QUERY_FEATURES = 2048
ROWS = 1024
ADAPTER_POOL = 128
N_REQ = 8


def placement_map(key):
    return jax.random.permutation(jax.random.fold_in(key, 201), ADAPTER_POOL).astype(jnp.int32)


def feature_ramp(low, high):
    position = jnp.arange(MODEL_WIDTH, dtype=jnp.float32) / (MODEL_WIDTH - 1.0)
    return jnp.exp(math.log(low) + (math.log(high) - math.log(low)) * position)


def draw_normed_hidden_rows(key, part):
    key = jax.random.fold_in(key, 6)
    key_noise, key_rough = jax.random.split(key, 2)
    rough = jnp.exp(jax.random.uniform(key_rough, (MODEL_WIDTH,), jnp.float32, math.log(0.7), math.log(1.4)))
    noise_part = jnp.clip(jax.random.normal(key_noise, (ROWS, MODEL_WIDTH), jnp.float32), -6.0, 6.0)
    scale_row = feature_ramp(0.4, 3.2) * rough
    return (noise_part * scale_row[None, :]).astype(jnp.bfloat16)


def draw_base_query_rows(key, part):
    key = jax.random.fold_in(key, 1)
    noise_part = jnp.clip(jax.random.normal(key, (ROWS, QUERY_FEATURES), jnp.float32), -6.0, 6.0)
    return noise_part.astype(jnp.bfloat16)


def draw_stored_keys(key, part):
    key = jax.random.fold_in(key, 2)
    noise_part = jnp.clip(jax.random.normal(key, (ROWS, CACHE, QUERY_FEATURES), jnp.float32), -6.0, 6.0)
    return (0.15 * noise_part).astype(jnp.bfloat16)


def draw_incoming_key(key, part):
    key = jax.random.fold_in(key, 7)
    noise_part = jnp.clip(jax.random.normal(key, (ROWS, QUERY_FEATURES), jnp.float32), -6.0, 6.0)
    return (0.15 * noise_part).astype(jnp.bfloat16)


def draw_cache_fill_length(key, part):
    key = jax.random.fold_in(key, 3)
    lengths = jax.random.randint(key, (ROWS,), 2, CACHE + 1, jnp.int32)
    first_rows = jnp.arange(ROWS, dtype=jnp.int32) % ROWS_DEV == 0
    return jnp.where(first_rows, CACHE, lengths).astype(jnp.int32)


def draw_adapter_pool_row(key, part):
    slot_index = placement_map(key)
    return slot_index


def draw_adapter_of_row(key, part):
    slot_index = placement_map(key)
    key = jax.random.fold_in(key, 5)
    key_offset, key_hot, key_other, key_local = jax.random.split(key, 4)
    hot_count = max(1, N_REQ // 8)
    offset = jax.random.randint(key_offset, (), 0, N_REQ, jnp.int32)
    hot_owner = (jax.random.randint(key_hot, (N_REQ,), 0, hot_count, jnp.int32) + offset) % N_REQ
    others = jax.vmap(lambda one_key: jax.random.permutation(one_key, N_REQ - 1))(jax.random.split(key_other, N_REQ)).astype(jnp.int32)
    position = jnp.arange(ROWS_DEV, dtype=jnp.int32)
    later_rows = jnp.maximum(position - CAP, 0) % (N_REQ - 1)
    spread = (hot_owner[:, None] + 1 + others[:, later_rows]) % N_REQ
    owner = jnp.where(position[None, :] < CAP, hot_owner[:, None], spread)
    local_slot = jax.random.randint(key_local, (N_REQ, ROWS_DEV), 0, ADAPT_DEV, jnp.int32)
    storage = (owner * ADAPT_DEV + local_slot).reshape(ROWS)
    inverse = jnp.zeros((ADAPTER_POOL,), jnp.int32).at[slot_index].set(jnp.arange(ADAPTER_POOL, dtype=jnp.int32))
    return inverse[storage]


def block_levels(key, extent, shards, least, top_value):
    def one(dim, blocks):
        heights = jax.random.uniform(jax.random.fold_in(jax.random.fold_in(key, 6), dim), (blocks,), jnp.float32, least / len(shards), top_value / len(shards))
        return jnp.repeat(jnp.exp(heights), extent[dim] // blocks).reshape((-1,) + (1,) * (len(extent) - dim - 1))

    gain = one(*shards[0])
    for cut in shards[1:]:
        gain = gain * one(*cut)
    return gain


def noise(key, shape, width, limit, shards=(), kind=jnp.bfloat16):
    entries = jax.random.normal(key, shape, jnp.float32) * width
    if len(shards) > 0:
        entries = block_levels(key, shape, shards, -0.22, 0.18) * entries
    return jnp.clip(entries, min=-limit, max=limit).astype(kind)


def setup_inputs(seed: int = 0, part: int = 0) -> dict:
    streams_of = jax.random.split(jax.random.key(seed), 16)
    own_keys = jax.random.split(jax.random.fold_in(streams_of[15], part), 16)
    return {
        "normed_hidden_rows": draw_normed_hidden_rows(jax.random.fold_in(jax.random.fold_in(streams_of[15], part), 71), part),
        "base_query_rows": draw_base_query_rows(jax.random.fold_in(jax.random.fold_in(streams_of[15], part), 71), part),
        "incoming_key": draw_incoming_key(jax.random.fold_in(jax.random.fold_in(streams_of[15], part), 71), part),
        "base_value_rows": noise(own_keys[3], (ROWS, QUERY_FEATURES), 0.3, 3.0, ((0, 8), (1, 2))),
        "stored_keys": draw_stored_keys(jax.random.fold_in(jax.random.fold_in(streams_of[15], part), 71), part),
        "stored_values": noise(own_keys[5], (ROWS, CACHE, QUERY_FEATURES), 0.3, 3.0, ((0, 8), (2, 2))),
        "cache_fill_length": draw_cache_fill_length(jax.random.fold_in(jax.random.fold_in(streams_of[15], part), 71), part),
        "adapter_of_row": draw_adapter_of_row(jax.random.fold_in(jax.random.fold_in(streams_of[15], part), 71), part),
        "adapter_pool_row": draw_adapter_pool_row(jax.random.fold_in(jax.random.fold_in(streams_of[15], part), 71), part),
        "output_projection_weight": noise(streams_of[9], (QUERY_FEATURES, MODEL_WIDTH), QUERY_FEATURES ** -0.5, 0.125, ((0, 2),)),
        "output_block_scales": jnp.clip(jnp.exp(math.log(2.0) - 1.3862944 * jax.random.uniform(streams_of[10], (QUERY_FEATURES // BLOCK, MODEL_WIDTH // BLOCK), jnp.float32) ** block_levels(streams_of[10], (QUERY_FEATURES // BLOCK, MODEL_WIDTH // BLOCK), ((0, 2),), -0.2, 0.2)), 0.5, 2.0),
        "query_value_down_maps": noise(streams_of[11], (ADAPTER_POOL, 2 * ADAPTER_RANK, MODEL_WIDTH), MODEL_WIDTH ** -0.5, 0.09375, ((0, 8),)),
        "query_value_up_maps": noise(streams_of[12], (ADAPTER_POOL, 2 * ADAPTER_RANK, QUERY_FEATURES), ADAPTER_RANK ** -0.5, 1.5, ((0, 8), (2, 2))),
        "output_down_maps": noise(streams_of[13], (ADAPTER_POOL, ADAPTER_RANK, QUERY_FEATURES), QUERY_FEATURES ** -0.5, 0.125, ((0, 8), (2, 2))),
        "output_up_maps": noise(streams_of[14], (ADAPTER_POOL, ADAPTER_RANK, MODEL_WIDTH), ADAPTER_RANK ** -0.5, 1.5, ((0, 8), (2, 2))),
    }


adapter_scale = 2.0

def reference(normed_hidden_rows, base_query_rows, incoming_key, base_value_rows, stored_keys, stored_values, cache_fill_length, adapter_of_row, adapter_pool_row, output_projection_weight, output_block_scales, query_value_down_maps, query_value_up_maps, output_down_maps, output_up_maps):
    slot_index = adapter_pool_row[adapter_of_row].astype(jnp.int32)

    def qv_row(item):
        values_per_row, single_pool_row = item
        rank_projection = jnp.dot(query_value_down_maps[single_pool_row], values_per_row, preferred_element_type=jnp.float32).astype(jnp.bfloat16)
        up_map_table = query_value_up_maps[single_pool_row]
        query_correction = (adapter_scale * jnp.dot(rank_projection[:ADAPTER_RANK], up_map_table[:ADAPTER_RANK], preferred_element_type=jnp.float32)).astype(jnp.bfloat16)
        value_correction = (adapter_scale * jnp.dot(rank_projection[ADAPTER_RANK:], up_map_table[ADAPTER_RANK:], preferred_element_type=jnp.float32)).astype(jnp.bfloat16)
        return (query_correction, value_correction)
    query_correction, value_correction = lax.map(qv_row, (normed_hidden_rows, slot_index))
    query_rows = (base_query_rows.astype(jnp.float32) + query_correction.astype(jnp.float32)).astype(jnp.bfloat16)
    value_new = (base_value_rows.astype(jnp.float32) + value_correction.astype(jnp.float32)).astype(jnp.bfloat16)
    inverse_root = 1.0 / math.sqrt(HEAD_DIM)
    query_heads = query_rows.reshape(ROWS, HEADS, HEAD_DIM).astype(jnp.float32)
    keys_heads = stored_keys.reshape(ROWS, CACHE, HEADS, HEAD_DIM).astype(jnp.float32)
    values_heads = stored_values.reshape(ROWS, CACHE, HEADS, HEAD_DIM).astype(jnp.float32)
    new_keys = incoming_key.reshape(ROWS, HEADS, HEAD_DIM).astype(jnp.float32)
    new_values = value_new.reshape(ROWS, HEADS, HEAD_DIM).astype(jnp.float32)
    scores = jnp.einsum('rhd,rphd->rhp', query_heads, keys_heads) * inverse_root
    own_score = jnp.einsum('rhd,rhd->rh', query_heads, new_keys) * inverse_root
    usable = jnp.arange(CACHE, dtype=jnp.int32)[None, :] < cache_fill_length[:, None]
    scores = jnp.where(usable[:, None, :], scores, -jnp.inf)
    highest = jnp.maximum(lax.optimization_barrier(jnp.max(scores, axis=-1)), own_score)
    cache_exp = jnp.exp(scores - highest[:, :, None])
    own_exp = jnp.exp(own_score - highest)
    denominator = lax.optimization_barrier(jnp.sum(cache_exp, axis=-1)) + own_exp
    weights = (cache_exp / denominator[:, :, None]).astype(jnp.bfloat16)
    own_weight = (own_exp / denominator).astype(jnp.bfloat16)
    context = jnp.einsum('rhp,rphd->rhd', weights.astype(jnp.float32), values_heads)
    context = context + own_weight.astype(jnp.float32)[:, :, None] * new_values
    context = context.astype(jnp.bfloat16).reshape(ROWS, QUERY_FEATURES)

    def o_row(item):
        context_per_row, single_pool_row = item
        rank_projection = jnp.dot(output_down_maps[single_pool_row], context_per_row, preferred_element_type=jnp.float32).astype(jnp.bfloat16)
        return (adapter_scale * jnp.dot(rank_projection, output_up_maps[single_pool_row], preferred_element_type=jnp.float32)).astype(jnp.bfloat16)
    output_correction = lax.map(o_row, (context, slot_index))
    base_terms = jnp.zeros((ROWS, MODEL_WIDTH), jnp.float32)
    for block_k in range(QUERY_FEATURES // BLOCK):
        lower = block_k * BLOCK
        product = jnp.dot(context[:, lower:lower + BLOCK], output_projection_weight[lower:lower + BLOCK], preferred_element_type=jnp.float32)
        base_terms = base_terms + product * jnp.repeat(output_block_scales[block_k], BLOCK)[None, :]
    return (base_terms + output_correction.astype(jnp.float32)).astype(jnp.bfloat16)
```

```python
import math

import jax
import jax.numpy as jnp
from jax import lax
from jax.experimental import pallas as pl
from jax.experimental.pallas import tpu as pltpu
from jax.sharding import PartitionSpec as P

HEAD_DIM = 128
ADAPTER_RANK = 16
BLOCK = 128
LANES = 128
GROUPS = 2
OUT_CHUNKS = 2
ROW_BLOCK = 16
F32 = jnp.float32
BF16 = jnp.bfloat16
adapter_scale = 2.0


def locate(adapter_of_row, adapter_pool_row, owners, adapter_spread, capacity):
    table_index = jnp.arange(adapter_pool_row.shape[0], dtype=jnp.int32)
    slot_index = jnp.sum(
        jnp.where(adapter_of_row[:, None] == table_index[None, :], adapter_pool_row[None, :], 0),
        axis=1,
    )
    owner = slot_index // adapter_spread
    local_slot = slot_index % adapter_spread
    row_count = adapter_of_row.shape[0]
    row_index = jnp.arange(row_count, dtype=jnp.int32)
    earlier = (owner[:, None] == owner[None, :]) & (row_index[None, :] < row_index[:, None])
    rank_in = jnp.sum(earlier.astype(jnp.int32), axis=1)
    place_index = owner * capacity + rank_in
    slots = jnp.arange(owners * capacity, dtype=jnp.int32)
    placing = (place_index[:, None] == slots[None, :]).astype(BF16)
    placing_t = (place_index[None, :] == slots[:, None]).astype(BF16)
    lanes = jnp.arange(LANES, dtype=jnp.int32)
    chosen = (local_slot[:, None] == lanes[None, :]).astype(BF16)
    return placing, placing_t, chosen


def dot(a, b):
    return jnp.dot(a, b, preferred_element_type=F32)


def dot_t(a, b):
    return lax.dot_general(a, b, (((1,), (1,)), ((), ())), preferred_element_type=F32)


def dot_split(a, b):
    high = a.astype(BF16)
    low = (a - high.astype(F32)).astype(BF16)
    return dot(high, b) + dot(low, b)


def indicator(shape, dim, width):
    wide = lax.broadcasted_iota(jnp.int32, shape, 1 - dim) // width
    narrow = lax.broadcasted_iota(jnp.int32, shape, dim)
    return (wide == narrow).astype(BF16)


def kernel(
    placing, placing_t, chosen, lengths, scales,
    hidden, base_q, key_in, base_v, keys, values, weight, down, up, o_down, o_up,
    out,
    hid_v, bq_v, kin_v, bv_v, keys_v, vals_v, w_v, down_v, up_v, odown_v, oup_v,
    x_send, x_recv, c_send, c_recv, t_send, t_recv, o_send, o_recv,
    sum_send, sum_recv, base_send, base_recv, base_own, q_v, vnew_v, ctx_v, mixed_v, omixed_v,
    local_sem, xs, xr, cs, cr, ts, tr, os_, or_, ps, pr,
):
    n, cap, _ = x_send.shape
    slots = n * cap
    half = hid_v.shape[1]
    rows, width = bq_v.shape
    group = width // GROUPS
    spread2 = mixed_v.shape[1]
    out_half = out.shape[1]
    out_chunk = out_half // OUT_CHUNKS
    me = lax.axis_index("req")
    tp = lax.axis_index("tp")
    other = 1 - tp

    def local(index, src, dst):
        return pltpu.make_async_copy(src, dst, local_sem.at[index])

    feature0 = pl.multiple_of(tp * half, half)
    loads = [
        local(0, hidden.at[:, pl.ds(feature0, half)], hid_v),
        local(1, down.at[:, :, pl.ds(feature0, half)], down_v),
        local(2, up, up_v),
        local(3, base_q, bq_v),
        local(4, base_v, bv_v),
        local(5, key_in, kin_v),
        local(6, keys, keys_v),
        local(7, values, vals_v),
        local(8, o_down, odown_v),
        local(9, weight, w_v),
        local(10, o_up, oup_v),
    ]
    for load in loads:
        load.start()

    barrier = pltpu.get_barrier_semaphore()

    @pl.loop(1, n)
    def _(d):
        pl.semaphore_signal(
            barrier, inc=1, device_id={"req": lax.rem(me + d, n)},
            device_id_type=pl.DeviceIdType.MESH,
        )

    pl.semaphore_signal(
        barrier, inc=1, device_id={"tp": other}, device_id_type=pl.DeviceIdType.MESH
    )

    def copy(send, recv, send_sem, recv_sem, d, slot):
        peer = lax.rem(me + d, n)
        return pltpu.make_async_remote_copy(
            src_ref=send.at[peer],
            dst_ref=recv.at[slot],
            send_sem=send_sem.at[d],
            recv_sem=recv_sem.at[d],
            device_id={"req": peer},
            device_id_type=pl.DeviceIdType.MESH,
        )

    def exchange(send, recv, send_sem, recv_sem):
        @pl.loop(1, n)
        def _(d):
            copy(send, recv, send_sem, recv_sem, d, me).start()

        recv[me] = send[me]

    def arrived(send, recv, send_sem, recv_sem):
        @pl.loop(1, n)
        def _(d):
            copy(send, recv, send_sem, recv_sem, d, lax.rem(me + n - d, n)).wait_recv()

    def sent(send, recv, send_sem, recv_sem):
        @pl.loop(1, n)
        def _(d):
            copy(send, recv, send_sem, recv_sem, d, me).wait_send()

    def sibling(index, src, dst):
        return pltpu.make_async_remote_copy(
            src_ref=src,
            dst_ref=dst,
            send_sem=ps.at[index],
            recv_sem=pr.at[index],
            device_id={"tp": other},
            device_id_type=pl.DeviceIdType.MESH,
        )

    loads[0].wait()
    tile = 512

    @pl.loop(0, half // tile)
    def _(t):
        cols = pl.ds(pl.multiple_of(t * tile, tile), tile)
        packed = dot(placing_t[...], hid_v[:, cols]).astype(BF16)
        x_send[:, :, cols] = packed.reshape(n, cap, tile)

    packed_chosen = dot(placing_t[...], chosen[...]).astype(BF16)
    x_send[:, :, half:] = packed_chosen.reshape(n, cap, LANES)
    pl.semaphore_wait(barrier, n)
    exchange(x_send, x_recv, xs, xr)
    loads[1].wait()
    loads[2].wait()
    arrived(x_send, x_recv, xs, xr)

    picked = x_recv[:, :, half:].reshape(slots, LANES)
    mask = dot(picked, indicator((LANES, spread2), 0, 2 * ADAPTER_RANK))
    shrink = dot_t(
        x_recv[:, :, :half].reshape(slots, half), down_v[...].reshape(spread2, half)
    )
    shrink = shrink * mask
    folded = shrink[:, :LANES]
    for t in range(1, spread2 // LANES):
        folded = folded + shrink[:, t * LANES : (t + 1) * LANES]
    sum_send[0] = folded
    swap = sibling(0, sum_send.at[0], sum_recv.at[0])
    swap.start()
    swap.wait()
    total = (sum_send[0] + sum_recv[0]).astype(BF16).astype(F32)
    mixed_v[...] = (jnp.concatenate([total] * (spread2 // LANES), axis=1) * mask).astype(BF16)

    up_rows = up_v.shape[0] * up_v.shape[1]
    rank_of = lax.broadcasted_iota(jnp.int32, (slots, spread2), 1) % (2 * ADAPTER_RANK)
    is_query = (rank_of < ADAPTER_RANK).astype(BF16)
    mixed_q = mixed_v[...] * is_query
    mixed_val = mixed_v[...] - mixed_q
    for g in range(GROUPS):
        cols = slice(g * group, (g + 1) * group)
        table = up_v[:, :, cols].reshape(up_rows, group)
        for which, mixed in ((0, mixed_q), (1, mixed_val)):
            corr = (adapter_scale * dot(mixed, table)).astype(BF16)
            c = 2 * g + which
            c_send[c] = corr.reshape(n, cap, group)
            exchange(c_send.at[c], c_recv.at[c], cs.at[c], cr.at[c])

    for index in range(3, 9):
        loads[index].wait()
    inverse_root = 1.0 / math.sqrt(HEAD_DIM)
    cache = keys_v.shape[1]
    gather = indicator((group, LANES), 1, HEAD_DIM)
    spreadm = indicator((LANES, group), 0, HEAD_DIM)
    position = lax.broadcasted_iota(jnp.int32, (ROW_BLOCK, cache, LANES), 1)
    for g in range(GROUPS):
        cols = slice(g * group, (g + 1) * group)
        for which, base, dest in ((0, bq_v, q_v), (1, bv_v, vnew_v)):
            c = 2 * g + which
            arrived(c_send.at[c], c_recv.at[c], cs.at[c], cr.at[c])
            corr = dot(placing[...], c_recv[c].reshape(slots, group))
            dest[:, cols] = (base[:, cols].astype(F32) + corr).astype(BF16)

        @pl.loop(0, rows // ROW_BLOCK)
        def _(i):
            block = pl.ds(pl.multiple_of(i * ROW_BLOCK, ROW_BLOCK), ROW_BLOCK)
            q = q_v[block, cols].astype(F32)
            product = keys_v[block, :, cols].astype(F32) * q[:, None, :]
            score = dot_split(product.reshape(ROW_BLOCK * cache, group), gather) * inverse_root
            score = score.reshape(ROW_BLOCK, cache, LANES)
            own = dot_split(q * kin_v[block, cols].astype(F32), gather) * inverse_root
            usable = position < lengths[block, :][:, None, :]
            score = jnp.where(usable, score, -jnp.inf)
            highest = jnp.maximum(jnp.max(score, axis=1), own)
            e = jnp.exp(score - highest[:, None, :])
            own_e = jnp.exp(own - highest)
            denominator = jnp.sum(e, axis=1) + own_e
            w = (e / denominator[:, None, :]).reshape(ROW_BLOCK * cache, LANES).astype(BF16)
            own_w = (own_e / denominator).astype(BF16)
            wide = dot(w, spreadm).reshape(ROW_BLOCK, cache, group)
            context = jnp.sum(wide * vals_v[block, :, cols].astype(F32), axis=1)
            context = context + dot(own_w, spreadm) * vnew_v[block, cols].astype(F32)
            ctx_v[block, cols] = context.astype(BF16)

        packed = dot(placing_t[...], ctx_v[:, cols]).astype(BF16)
        t_send[g] = packed.reshape(n, cap, group)
        exchange(t_send.at[g], t_recv.at[g], ts.at[g], tr.at[g])

    loads[9].wait()
    loads[10].wait()

    def project(column):
        total = None
        for k in range(width // BLOCK):
            part = dot(ctx_v[:, k * BLOCK : (k + 1) * BLOCK], w_v[k * BLOCK : (k + 1) * BLOCK, column])
            part = part * scales[k : k + 1, column]
            total = part if total is None else total + part
        return total

    @pl.loop(0, out_half // tile)
    def _(t):
        column = pl.ds(pl.multiple_of(other * out_half + t * tile, tile), tile)
        base_send[:, pl.ds(pl.multiple_of(t * tile, tile), tile)] = project(column)

    base_swap = sibling(2, base_send, base_recv)

    omask = dot(picked, indicator((LANES, omixed_v.shape[1]), 0, ADAPTER_RANK))
    orows = odown_v.shape[0] * odown_v.shape[1]
    oshrink = None
    for g in range(GROUPS):
        arrived(t_send.at[g], t_recv.at[g], ts.at[g], tr.at[g])
        part = dot_t(
            t_recv[g].reshape(slots, group),
            odown_v[:, :, g * group : (g + 1) * group].reshape(orows, group),
        )
        oshrink = part if oshrink is None else oshrink + part
    oshrink = oshrink * omask
    ofolded = oshrink[:, :LANES]
    for t in range(1, orows // LANES):
        ofolded = ofolded + oshrink[:, t * LANES : (t + 1) * LANES]
    sum_send[1] = ofolded
    oswap = sibling(1, sum_send.at[1], sum_recv.at[1])
    oswap.start()
    oswap.wait()
    base_swap.start()
    ototal = (sum_send[1] + sum_recv[1]).astype(BF16).astype(F32)
    omixed_v[...] = (jnp.concatenate([ototal] * (orows // LANES), axis=1) * omask).astype(BF16)
    for c in range(OUT_CHUNKS):
        table = oup_v[:, :, c * out_chunk : (c + 1) * out_chunk].reshape(orows, out_chunk)
        corr = (adapter_scale * dot(omixed_v[...], table)).astype(BF16)
        o_send[c] = corr.reshape(n, cap, out_chunk)
        exchange(o_send.at[c], o_recv.at[c], os_.at[c], or_.at[c])

    @pl.loop(0, out_half // tile)
    def _(t):
        column = pl.ds(pl.multiple_of(tp * out_half + t * tile, tile), tile)
        base_own[:, pl.ds(pl.multiple_of(t * tile, tile), tile)] = project(column)

    base_swap.wait()
    for c in range(OUT_CHUNKS):
        cols = slice(c * out_chunk, (c + 1) * out_chunk)
        arrived(o_send.at[c], o_recv.at[c], os_.at[c], or_.at[c])
        corr = dot(placing[...], o_recv[c].reshape(slots, out_chunk))
        out[:, cols] = (base_own[:, cols] + base_recv[:, cols] + corr).astype(BF16)

    sent(x_send, x_recv, xs, xr)
    for c in range(2 * GROUPS):
        sent(c_send.at[c], c_recv.at[c], cs.at[c], cr.at[c])
    for g in range(GROUPS):
        sent(t_send.at[g], t_recv.at[g], ts.at[g], tr.at[g])
    for c in range(OUT_CHUNKS):
        sent(o_send.at[c], o_recv.at[c], os_.at[c], or_.at[c])


def shards(
    normed_hidden_rows,
    base_query_rows,
    incoming_key,
    base_value_rows,
    stored_keys,
    stored_values,
    cache_fill_length,
    adapter_of_row,
    adapter_pool_row,
    output_projection_weight,
    output_block_scales,
    query_value_down_maps,
    query_value_up_maps,
    output_down_maps,
    output_up_maps,
):
    n = lax.axis_size("req")
    spread = query_value_down_maps.shape[0]
    rows, model_width = normed_hidden_rows.shape
    width = base_query_rows.shape[1]
    cap = max(16, 2 * ((rows + n - 1) // n))
    slots = n * cap
    half = model_width // lax.axis_size("tp")
    out_half = output_up_maps.shape[2]
    group = width // GROUPS
    out_chunk = out_half // OUT_CHUNKS
    placing, placing_t, chosen = locate(adapter_of_row, adapter_pool_row, n, spread, cap)
    lengths = jnp.broadcast_to(cache_fill_length[:, None], (rows, LANES))
    scales = jnp.repeat(output_block_scales, BLOCK, axis=1)
    vmem = pl.BlockSpec(memory_space=pltpu.VMEM)
    hbm = pl.BlockSpec(memory_space=pl.ANY)

    def like(x):
        return pltpu.VMEM(x.shape, x.dtype)

    dma = pltpu.SemaphoreType.DMA
    return pl.pallas_call(
        kernel,
        out_shape=jax.ShapeDtypeStruct((rows, out_half), BF16),
        in_specs=[vmem] * 5 + [hbm] * 11,
        out_specs=vmem,
        scratch_shapes=[
            pltpu.VMEM((rows, half), BF16),
            like(base_query_rows),
            like(incoming_key),
            like(base_value_rows),
            like(stored_keys),
            like(stored_values),
            like(output_projection_weight),
            pltpu.VMEM((spread, query_value_down_maps.shape[1], half), BF16),
            like(query_value_up_maps),
            like(output_down_maps),
            like(output_up_maps),
            pltpu.VMEM((n, cap, half + LANES), BF16),
            pltpu.VMEM((n, cap, half + LANES), BF16),
            pltpu.VMEM((2 * GROUPS, n, cap, group), BF16),
            pltpu.VMEM((2 * GROUPS, n, cap, group), BF16),
            pltpu.VMEM((GROUPS, n, cap, group), BF16),
            pltpu.VMEM((GROUPS, n, cap, group), BF16),
            pltpu.VMEM((OUT_CHUNKS, n, cap, out_chunk), BF16),
            pltpu.VMEM((OUT_CHUNKS, n, cap, out_chunk), BF16),
            pltpu.VMEM((2, slots, LANES), F32),
            pltpu.VMEM((2, slots, LANES), F32),
            pltpu.VMEM((rows, out_half), F32),
            pltpu.VMEM((rows, out_half), F32),
            pltpu.VMEM((rows, out_half), F32),
            pltpu.VMEM((rows, width), BF16),
            pltpu.VMEM((rows, width), BF16),
            pltpu.VMEM((rows, width), BF16),
            pltpu.VMEM((slots, spread * 2 * ADAPTER_RANK), BF16),
            pltpu.VMEM((slots, spread * ADAPTER_RANK), BF16),
            dma((11,)),
            dma((n,)),
            dma((n,)),
            dma((2 * GROUPS, n)),
            dma((2 * GROUPS, n)),
            dma((GROUPS, n)),
            dma((GROUPS, n)),
            dma((OUT_CHUNKS, n)),
            dma((OUT_CHUNKS, n)),
            dma((3,)),
            dma((3,)),
        ],
        compiler_params=pltpu.CompilerParams(
            collective_id=0, has_side_effects=True, vmem_limit_bytes=58 * 1024 * 1024
        ),
    )(
        placing, placing_t, chosen, lengths, scales,
        normed_hidden_rows, base_query_rows, incoming_key, base_value_rows,
        stored_keys, stored_values, output_projection_weight,
        query_value_down_maps, query_value_up_maps, output_down_maps, output_up_maps,
    )


def solution(mesh):
    in_specs = (
        P(("replica", "req"), None),
        P(("replica", "req"), "tp"),
        P(("replica", "req"), "tp"),
        P(("replica", "req"), "tp"),
        P(("replica", "req"), None, "tp"),
        P(("replica", "req"), None, "tp"),
        P(("replica", "req")),
        P(("replica", "req")),
        P("replica"),
        P("tp", None),
        P("tp", None),
        P("req", None, None),
        P("req", None, "tp"),
        P("req", None, "tp"),
        P("req", None, "tp"),
    )
    out_specs = P(("replica", "req"), "tp")
    return jax.shard_map(shards, mesh=mesh, in_specs=in_specs, out_specs=out_specs, check_vma=False)
```

```python
import math

import jax
import jax.numpy as jnp
from jax import lax
from jax.experimental import pallas as pl
from jax.experimental.pallas import tpu as pltpu
from jax.sharding import PartitionSpec as P

HEAD_DIM = 128
ADAPTER_RANK = 16
BLOCK = 128
LANES = 128
GROUPS = 2
OUT_CHUNKS = 2
ROW_BLOCK = 32
SUB = 16
F32 = jnp.float32
BF16 = jnp.bfloat16
adapter_scale = 2.0


def dot(a, b):
    return jnp.dot(a, b, preferred_element_type=F32)


def dot_t(a, b):
    return lax.dot_general(a, b, (((1,), (1,)), ((), ())), preferred_element_type=F32)


def dot_split(a, b):
    high = a.astype(BF16)
    low = (a - high.astype(F32)).astype(BF16)
    return dot(high, b) + dot(low, b)


def indicator(shape, dim, width):
    wide = lax.broadcasted_iota(jnp.int32, shape, 1 - dim) // width
    narrow = lax.broadcasted_iota(jnp.int32, shape, dim)
    return (wide == narrow).astype(BF16)


def column(row):
    return jnp.transpose(jnp.broadcast_to(row, (LANES, LANES)))


def kernel(
    adapter_of_row, adapter_pool_row, fill, scales,
    hidden, base_q, key_in, base_v, keys, values, weight, down, up, o_down, o_up,
    out,
    hid_v, bq_v, kin_v, bv_v, keys_v, vals_v, w_v, down_v, up_v, odown_v, oup_v,
    placing, placing_t, lengths, wide_scales,
    x_send, x_recv, c_send, c_recv, t_send, t_recv, o_send, o_recv,
    sum_send, sum_recv, base_send, base_recv, base_own, q_v, vnew_v, ctx_v, mixed_v, omixed_v,
    local_sem, xs, xr, cs, cr, ts, tr, os_, or_, ps, pr,
):
    halves, n, sub, _ = x_send.shape
    part = n * sub
    half = hid_v.shape[1]
    rows, width = bq_v.shape
    group = width // GROUPS
    spread = odown_v.shape[0]
    spread2 = mixed_v.shape[2]
    orows = omixed_v.shape[2]
    out_half = out.shape[1]
    out_chunk = out_half // OUT_CHUNKS
    me = lax.axis_index("req")
    tp = lax.axis_index("tp")
    other = 1 - tp

    def local(index, src, dst):
        return pltpu.make_async_copy(src, dst, local_sem.at[index])

    feature0 = pl.multiple_of(tp * half, half)
    loads = [
        local(0, hidden.at[:, pl.ds(feature0, half)], hid_v),
        local(1, down.at[:, :, pl.ds(feature0, half)], down_v),
        local(2, up, up_v),
        local(3, base_q, bq_v),
        local(4, base_v, bv_v),
        local(5, key_in, kin_v),
        local(6, keys, keys_v),
        local(7, values, vals_v),
        local(8, o_down, odown_v),
        local(9, weight, w_v),
        local(10, o_up, oup_v),
    ]
    loads[0].start()

    barrier = pltpu.get_barrier_semaphore()

    @pl.loop(1, n)
    def _(d):
        pl.semaphore_signal(
            barrier, inc=1, device_id={"req": lax.rem(me + d, n)},
            device_id_type=pl.DeviceIdType.MESH,
        )

    pl.semaphore_signal(
        barrier, inc=1, device_id={"tp": other}, device_id_type=pl.DeviceIdType.MESH
    )

    def copy(send, recv, send_sem, recv_sem, d, slot):
        peer = lax.rem(me + d, n)
        return pltpu.make_async_remote_copy(
            src_ref=send.at[peer],
            dst_ref=recv.at[slot],
            send_sem=send_sem.at[d],
            recv_sem=recv_sem.at[d],
            device_id={"req": peer},
            device_id_type=pl.DeviceIdType.MESH,
        )

    def exchange(send, recv, send_sem, recv_sem):
        @pl.loop(1, n)
        def _(d):
            copy(send, recv, send_sem, recv_sem, d, me).start()

        recv[me] = send[me]

    def arrived(send, recv, send_sem, recv_sem):
        @pl.loop(1, n)
        def _(d):
            copy(send, recv, send_sem, recv_sem, d, lax.rem(me + n - d, n)).wait_recv()

    def sent(send, recv, send_sem, recv_sem):
        @pl.loop(1, n)
        def _(d):
            copy(send, recv, send_sem, recv_sem, d, me).wait_send()

    def hidden_move(h):
        return x_send.at[h], x_recv.at[h], xs.at[h], xr.at[h]

    def corr_move(g, h):
        i = g * halves + h
        return c_send.at[i], c_recv.at[i], cs.at[i], cr.at[i]

    def context_move(g, h):
        i = g * halves + h
        return t_send.at[i], t_recv.at[i], ts.at[i], tr.at[i]

    def out_move(h, c):
        i = h * OUT_CHUNKS + c
        return o_send.at[i], o_recv.at[i], os_.at[i], or_.at[i]

    def sibling(index, src, dst):
        return pltpu.make_async_remote_copy(
            src_ref=src,
            dst_ref=dst,
            send_sem=ps.at[index],
            recv_sem=pr.at[index],
            device_id={"tp": other},
            device_id_type=pl.DeviceIdType.MESH,
        )

    pool = adapter_pool_row.shape[1]
    named = lax.broadcasted_iota(jnp.int32, (pool, rows), 0) == adapter_of_row[...]
    named = named.astype(F32).astype(BF16)
    stored = jnp.broadcast_to(adapter_pool_row[...], (16, pool))
    owner = dot((stored // spread).astype(F32).astype(BF16), named)[:1]
    local_slot = dot((stored % spread).astype(F32).astype(BF16), named)[:1]
    lower = lax.broadcasted_iota(jnp.int32, (rows, rows), 0) < lax.broadcasted_iota(
        jnp.int32, (rows, rows), 1
    )
    earlier = (column(owner) == owner) & lower
    rank = jnp.sum(earlier.astype(F32), axis=0, keepdims=True).astype(jnp.int32)
    place = (rank // sub) * part + owner.astype(jnp.int32) * sub + rank % sub
    slots = halves * part
    placing_t[...] = (
        (lax.broadcasted_iota(jnp.int32, (slots, rows), 0) == place).astype(F32).astype(BF16)
    )
    place_c = column(place.astype(F32)).astype(jnp.int32)
    lane = lax.broadcasted_iota(jnp.int32, (rows, LANES), 1)
    for t in range(slots // LANES):
        here = (lane + t * LANES == place_c).astype(F32).astype(BF16)
        placing[:, t * LANES : (t + 1) * LANES] = here
    chosen = (lane == column(local_slot).astype(jnp.int32)).astype(F32).astype(BF16)
    lengths[...] = column(fill[...].astype(F32)).astype(jnp.int32)

    loads[0].wait()
    for load in loads[1:4]:
        load.start()
    tile = 512
    for h in range(halves):
        pick = slice(h * part, (h + 1) * part)

        @pl.loop(0, half // tile)
        def _(t):
            cols = pl.ds(pl.multiple_of(t * tile, tile), tile)
            packed = dot(placing_t[pick], hid_v[:, cols]).astype(BF16)
            x_send[h, :, :, cols] = packed.reshape(n, sub, tile)

        packed_chosen = dot(placing_t[pick], chosen).astype(BF16)
        x_send[h, :, :, half:] = packed_chosen.reshape(n, sub, LANES)
        if h == 0:
            pl.semaphore_wait(barrier, n)
        exchange(*hidden_move(h))
    for load in loads[4:]:
        load.start()

    high = scales[...].astype(BF16)
    rest = scales[...] - high.astype(F32)
    middle = rest.astype(BF16)
    low = (rest - middle.astype(F32)).astype(BF16)
    blocks = scales.shape[1]
    block_of = lax.broadcasted_iota(jnp.int32, (blocks, tile), 0)
    block_at = lax.broadcasted_iota(jnp.int32, (blocks, tile), 1) // BLOCK
    for t in range(wide_scales.shape[1] // tile):
        chosen_block = (block_of == block_at + t * (tile // BLOCK)).astype(F32).astype(BF16)
        wide_scales[:, t * tile : (t + 1) * tile] = (
            dot(high, chosen_block) + dot(middle, chosen_block) + dot(low, chosen_block)
        )

    loads[1].wait()
    loads[2].wait()

    def sum_cores(index, shrink, mask):
        pieces = shrink.shape[1] // LANES
        shrink = shrink * mask
        folded = shrink[:, :LANES]
        for t in range(1, pieces):
            folded = folded + shrink[:, t * LANES : (t + 1) * LANES]
        sum_send[index] = folded
        swap = sibling(index, sum_send.at[index], sum_recv.at[index])
        swap.start()
        swap.wait()
        total = (sum_send[index] + sum_recv[index]).astype(BF16).astype(F32)
        return (jnp.concatenate([total] * pieces, axis=1) * mask).astype(BF16)

    def picked(h):
        return x_recv[h, :, :, half:].reshape(part, LANES)

    rank_of = lax.broadcasted_iota(jnp.int32, (part, spread2), 1) % (2 * ADAPTER_RANK)
    is_query = (rank_of < ADAPTER_RANK).astype(F32).astype(BF16)

    def correct(g, h):
        mixed = mixed_v[h]
        mixed_q = mixed * is_query
        table = up_v[:, :, g * group : (g + 1) * group].reshape(spread2, group)
        i = g * halves + h
        corr = (adapter_scale * dot(mixed_q, table)).astype(BF16)
        c_send[i, :, :, :group] = corr.reshape(n, sub, group)
        corr = (adapter_scale * dot(mixed - mixed_q, table)).astype(BF16)
        c_send[i, :, :, group:] = corr.reshape(n, sub, group)
        exchange(*corr_move(g, h))

    for h in range(halves):
        arrived(*hidden_move(h))
        mask = dot(picked(h), indicator((LANES, spread2), 0, 2 * ADAPTER_RANK))
        shrink = dot_t(
            x_recv[h, :, :, :half].reshape(part, half), down_v[...].reshape(spread2, half)
        )
        mixed_v[h] = sum_cores(h, shrink, mask)
        correct(0, h)
    for g in range(1, GROUPS):
        for h in range(halves):
            correct(g, h)

    for index in range(3, 9):
        loads[index].wait()
    inverse_root = 1.0 / math.sqrt(HEAD_DIM)
    cache = keys_v.shape[1]
    gather = indicator((group, LANES), 1, HEAD_DIM)
    spreadm = indicator((LANES, group), 0, HEAD_DIM)
    position = lax.broadcasted_iota(jnp.int32, (ROW_BLOCK, cache, LANES), 1)
    for g in range(GROUPS):
        cols = slice(g * group, (g + 1) * group)
        corr = None
        for h in range(halves):
            arrived(*corr_move(g, h))
            term = dot(
                placing[:, h * part : (h + 1) * part],
                c_recv[g * halves + h].reshape(part, 2 * group),
            )
            corr = term if corr is None else corr + term
        q_v[:, cols] = (bq_v[:, cols].astype(F32) + corr[:, :group]).astype(BF16)
        vnew_v[:, cols] = (bv_v[:, cols].astype(F32) + corr[:, group:]).astype(BF16)

        @pl.loop(0, rows // ROW_BLOCK)
        def _(i):
            block = pl.ds(pl.multiple_of(i * ROW_BLOCK, ROW_BLOCK), ROW_BLOCK)
            q = q_v[block, cols].astype(F32)
            product = keys_v[block, :, cols].astype(F32) * q[:, None, :]
            score = dot_split(product.reshape(ROW_BLOCK * cache, group), gather) * inverse_root
            score = score.reshape(ROW_BLOCK, cache, LANES)
            own = dot_split(q * kin_v[block, cols].astype(F32), gather) * inverse_root
            usable = position < lengths[block, :][:, None, :]
            score = jnp.where(usable, score, -jnp.inf)
            highest = jnp.maximum(jnp.max(score, axis=1), own)
            e = jnp.exp(score - highest[:, None, :])
            own_e = jnp.exp(own - highest)
            denominator = jnp.sum(e, axis=1) + own_e
            w = (e / denominator[:, None, :]).reshape(ROW_BLOCK * cache, LANES).astype(BF16)
            own_w = (own_e / denominator).astype(BF16)
            wide = dot(w, spreadm).reshape(ROW_BLOCK, cache, group)
            context = jnp.sum(wide * vals_v[block, :, cols].astype(F32), axis=1)
            context = context + dot(own_w, spreadm) * vnew_v[block, cols].astype(F32)
            ctx_v[block, cols] = context.astype(BF16)

        for h in range(halves):
            packed = dot(placing_t[h * part : (h + 1) * part], ctx_v[:, cols]).astype(BF16)
            t_send[g * halves + h] = packed.reshape(n, sub, group)
            exchange(*context_move(g, h))

    loads[9].wait()
    loads[10].wait()

    def project(columns):
        total = None
        for k in range(width // BLOCK):
            span = slice(k * BLOCK, (k + 1) * BLOCK)
            term = dot(ctx_v[:, span], w_v[span, columns]) * wide_scales[k : k + 1, columns]
            total = term if total is None else total + term
        return total

    @pl.loop(0, out_half // tile)
    def _(t):
        columns = pl.ds(pl.multiple_of(other * out_half + t * tile, tile), tile)
        base_send[:, pl.ds(pl.multiple_of(t * tile, tile), tile)] = project(columns)

    base_swap = sibling(2 * halves, base_send, base_recv)

    for h in range(halves):
        omask = dot(picked(h), indicator((LANES, orows), 0, ADAPTER_RANK))
        oshrink = None
        for g in range(GROUPS):
            arrived(*context_move(g, h))
            term = dot_t(
                t_recv[g * halves + h].reshape(part, group),
                odown_v[:, :, g * group : (g + 1) * group].reshape(orows, group),
            )
            oshrink = term if oshrink is None else oshrink + term
        omixed_v[h] = sum_cores(halves + h, oshrink, omask)
        for c in range(OUT_CHUNKS):
            table = oup_v[:, :, c * out_chunk : (c + 1) * out_chunk].reshape(orows, out_chunk)
            corr = (adapter_scale * dot(omixed_v[h], table)).astype(BF16)
            o_send[h * OUT_CHUNKS + c] = corr.reshape(n, sub, out_chunk)
            exchange(*out_move(h, c))
    base_swap.start()

    @pl.loop(0, out_half // tile)
    def _(t):
        columns = pl.ds(pl.multiple_of(tp * out_half + t * tile, tile), tile)
        base_own[:, pl.ds(pl.multiple_of(t * tile, tile), tile)] = project(columns)

    base_swap.wait()
    for h in range(halves):
        for c in range(OUT_CHUNKS):
            cols = slice(c * out_chunk, (c + 1) * out_chunk)
            arrived(*out_move(h, c))
            total = base_own[:, cols] + dot(
                placing[:, h * part : (h + 1) * part],
                o_recv[h * OUT_CHUNKS + c].reshape(part, out_chunk),
            )
            if h == 0:
                total = total + base_recv[:, cols]
            if h == halves - 1:
                out[:, cols] = total.astype(BF16)
            else:
                base_own[:, cols] = total

    for h in range(halves):
        sent(*hidden_move(h))
        for g in range(GROUPS):
            sent(*corr_move(g, h))
            sent(*context_move(g, h))
        for c in range(OUT_CHUNKS):
            sent(*out_move(h, c))


def shards(
    normed_hidden_rows,
    base_query_rows,
    incoming_key,
    base_value_rows,
    stored_keys,
    stored_values,
    cache_fill_length,
    adapter_of_row,
    adapter_pool_row,
    output_projection_weight,
    output_block_scales,
    query_value_down_maps,
    query_value_up_maps,
    output_down_maps,
    output_up_maps,
):
    n = lax.axis_size("req")
    spread = query_value_down_maps.shape[0]
    rows, model_width = normed_hidden_rows.shape
    width = base_query_rows.shape[1]
    halves = (2 * ((rows + n - 1) // n) + SUB - 1) // SUB
    part = n * SUB
    slots = halves * part
    half = model_width // lax.axis_size("tp")
    out_half = output_up_maps.shape[2]
    group = width // GROUPS
    out_chunk = out_half // OUT_CHUNKS
    vmem = pl.BlockSpec(memory_space=pltpu.VMEM)
    hbm = pl.BlockSpec(memory_space=pl.ANY)

    def like(x):
        return pltpu.VMEM(x.shape, x.dtype)

    dma = pltpu.SemaphoreType.DMA
    return pl.pallas_call(
        kernel,
        out_shape=jax.ShapeDtypeStruct((rows, out_half), BF16),
        in_specs=[vmem] * 4 + [hbm] * 11,
        out_specs=vmem,
        scratch_shapes=[
            pltpu.VMEM((rows, half), BF16),
            like(base_query_rows),
            like(incoming_key),
            like(base_value_rows),
            like(stored_keys),
            like(stored_values),
            like(output_projection_weight),
            pltpu.VMEM((spread, query_value_down_maps.shape[1], half), BF16),
            like(query_value_up_maps),
            like(output_down_maps),
            like(output_up_maps),
            pltpu.VMEM((rows, slots), BF16),
            pltpu.VMEM((slots, rows), BF16),
            pltpu.VMEM((rows, LANES), jnp.int32),
            pltpu.VMEM((output_block_scales.shape[0], model_width), F32),
            pltpu.VMEM((halves, n, SUB, half + LANES), BF16),
            pltpu.VMEM((halves, n, SUB, half + LANES), BF16),
            pltpu.VMEM((GROUPS * halves, n, SUB, 2 * group), BF16),
            pltpu.VMEM((GROUPS * halves, n, SUB, 2 * group), BF16),
            pltpu.VMEM((GROUPS * halves, n, SUB, group), BF16),
            pltpu.VMEM((GROUPS * halves, n, SUB, group), BF16),
            pltpu.VMEM((OUT_CHUNKS * halves, n, SUB, out_chunk), BF16),
            pltpu.VMEM((OUT_CHUNKS * halves, n, SUB, out_chunk), BF16),
            pltpu.VMEM((2 * halves, part, LANES), F32),
            pltpu.VMEM((2 * halves, part, LANES), F32),
            pltpu.VMEM((rows, out_half), F32),
            pltpu.VMEM((rows, out_half), F32),
            pltpu.VMEM((rows, out_half), F32),
            pltpu.VMEM((rows, width), BF16),
            pltpu.VMEM((rows, width), BF16),
            pltpu.VMEM((rows, width), BF16),
            pltpu.VMEM((halves, part, spread * 2 * ADAPTER_RANK), BF16),
            pltpu.VMEM((halves, part, spread * ADAPTER_RANK), BF16),
            dma((11,)),
            dma((halves, n)),
            dma((halves, n)),
            dma((GROUPS * halves, n)),
            dma((GROUPS * halves, n)),
            dma((GROUPS * halves, n)),
            dma((GROUPS * halves, n)),
            dma((OUT_CHUNKS * halves, n)),
            dma((OUT_CHUNKS * halves, n)),
            dma((2 * halves + 1,)),
            dma((2 * halves + 1,)),
        ],
        compiler_params=pltpu.CompilerParams(
            collective_id=0, has_side_effects=True, vmem_limit_bytes=58 * 1024 * 1024
        ),
    )(
        adapter_of_row[None, :], adapter_pool_row[None, :], cache_fill_length[None, :],
        output_block_scales, normed_hidden_rows, base_query_rows, incoming_key, base_value_rows,
        stored_keys, stored_values, output_projection_weight,
        query_value_down_maps, query_value_up_maps, output_down_maps, output_up_maps,
    )


def solution(mesh):
    in_specs = (
        P(("replica", "req"), None),
        P(("replica", "req"), "tp"),
        P(("replica", "req"), "tp"),
        P(("replica", "req"), "tp"),
        P(("replica", "req"), None, "tp"),
        P(("replica", "req"), None, "tp"),
        P(("replica", "req")),
        P(("replica", "req")),
        P("replica"),
        P("tp", None),
        P("tp", None),
        P("req", None, None),
        P("req", None, "tp"),
        P("req", None, "tp"),
        P("req", None, "tp"),
    )
    out_specs = P(("replica", "req"), "tp")
    return jax.shard_map(shards, mesh=mesh, in_specs=in_specs, out_specs=out_specs, check_vma=False)
```

```python
import math

import jax
import jax.numpy as jnp
from jax import lax
from jax.experimental import pallas as pl
from jax.experimental.pallas import tpu as pltpu
from jax.sharding import PartitionSpec as P

HEAD_DIM = 128
ADAPTER_RANK = 16
BLOCK = 128
LANES = 128
GROUPS = 2
OUT_CHUNKS = 1
ROW_BLOCK = 64
SUB = 16
F32 = jnp.float32
BF16 = jnp.bfloat16
adapter_scale = 2.0


def dot(a, b):
    return jnp.dot(a, b, preferred_element_type=F32)


def dot_t(a, b):
    return lax.dot_general(a, b, (((1,), (1,)), ((), ())), preferred_element_type=F32)


def dot_split(a, b):
    high = a.astype(BF16)
    low = (a - high.astype(F32)).astype(BF16)
    return dot(high, b) + dot(low, b)


def indicator(shape, dim, width):
    wide = lax.broadcasted_iota(jnp.int32, shape, 1 - dim) // width
    narrow = lax.broadcasted_iota(jnp.int32, shape, dim)
    return (wide == narrow).astype(BF16)


def column(row):
    return jnp.transpose(jnp.broadcast_to(row, (LANES, LANES)))


def kernel(
    adapter_of_row, adapter_pool_row, fill, scales,
    hidden, base_q, key_in, base_v, keys, values, weight, down, up, o_down, o_up,
    out,
    hid_v, bq_v, kin_v, bv_v, keys_v, vals_v, w_v, down_v, up_v, odown_v, oup_v,
    placing, placing_t, lengths, wide_scales,
    x_send, x_recv, c_send, c_recv, t_send, t_recv, o_send, o_recv,
    sum_send, sum_recv, base_send, base_recv, base_own, q_v, vnew_v, ctx_v, mixed_v, omixed_v,
    local_sem, xs, xr, cs, cr, ts, tr, os_, or_, ps, pr,
):
    halves, n, sub, _ = x_send.shape
    part = n * sub
    half = hid_v.shape[1]
    rows, width = bq_v.shape
    group = width // GROUPS
    spread = odown_v.shape[0]
    spread2 = mixed_v.shape[2]
    orows = omixed_v.shape[2]
    out_half = out.shape[1]
    out_chunk = out_half // OUT_CHUNKS
    me = lax.axis_index("req")
    tp = lax.axis_index("tp")
    other = 1 - tp

    def local(index, src, dst):
        return pltpu.make_async_copy(src, dst, local_sem.at[index])

    feature0 = pl.multiple_of(tp * half, half)
    loads = [
        local(0, hidden.at[:, pl.ds(feature0, half)], hid_v),
        local(1, down.at[:, :, pl.ds(feature0, half)], down_v),
        local(2, up, up_v),
        local(3, base_q, bq_v),
        local(4, base_v, bv_v),
        local(5, key_in, kin_v),
        local(6, keys, keys_v),
        local(7, values, vals_v),
        local(8, o_down, odown_v),
        local(9, weight, w_v),
        local(10, o_up, oup_v),
    ]
    loads[0].start()

    barrier = pltpu.get_barrier_semaphore()

    @pl.loop(1, n)
    def _(d):
        pl.semaphore_signal(
            barrier, inc=1, device_id={"req": lax.rem(me + d, n)},
            device_id_type=pl.DeviceIdType.MESH,
        )

    pl.semaphore_signal(
        barrier, inc=1, device_id={"tp": other}, device_id_type=pl.DeviceIdType.MESH
    )

    def copy(send, recv, send_sem, recv_sem, d, slot):
        peer = lax.rem(me + d, n)
        return pltpu.make_async_remote_copy(
            src_ref=send.at[peer],
            dst_ref=recv.at[slot],
            send_sem=send_sem.at[d],
            recv_sem=recv_sem.at[d],
            device_id={"req": peer},
            device_id_type=pl.DeviceIdType.MESH,
        )

    def exchange(send, recv, send_sem, recv_sem):
        @pl.loop(1, n)
        def _(d):
            copy(send, recv, send_sem, recv_sem, d, me).start()

        recv[me] = send[me]

    def arrived(send, recv, send_sem, recv_sem):
        @pl.loop(1, n)
        def _(d):
            copy(send, recv, send_sem, recv_sem, d, lax.rem(me + n - d, n)).wait_recv()

    def sent(send, recv, send_sem, recv_sem):
        @pl.loop(1, n)
        def _(d):
            copy(send, recv, send_sem, recv_sem, d, me).wait_send()

    def hidden_move(h):
        return x_send.at[h], x_recv.at[h], xs.at[h], xr.at[h]

    def corr_move(g, h):
        i = g * halves + h
        return c_send.at[i], c_recv.at[i], cs.at[i], cr.at[i]

    def context_move(g, h):
        i = g * halves + h
        return t_send.at[i], t_recv.at[i], ts.at[i], tr.at[i]

    def out_move(h, c):
        i = h * OUT_CHUNKS + c
        return o_send.at[i], o_recv.at[i], os_.at[i], or_.at[i]

    def sibling(index, src, dst):
        return pltpu.make_async_remote_copy(
            src_ref=src,
            dst_ref=dst,
            send_sem=ps.at[index],
            recv_sem=pr.at[index],
            device_id={"tp": other},
            device_id_type=pl.DeviceIdType.MESH,
        )

    pool = adapter_pool_row.shape[1]
    named = lax.broadcasted_iota(jnp.int32, (pool, rows), 0) == adapter_of_row[...]
    named = named.astype(F32).astype(BF16)
    stored = jnp.broadcast_to(adapter_pool_row[...], (16, pool))
    owner = dot((stored // spread).astype(F32).astype(BF16), named)[:1]
    local_slot = dot((stored % spread).astype(F32).astype(BF16), named)[:1]
    lower = lax.broadcasted_iota(jnp.int32, (rows, rows), 0) < lax.broadcasted_iota(
        jnp.int32, (rows, rows), 1
    )
    earlier = (column(owner) == owner) & lower
    rank = jnp.sum(earlier.astype(F32), axis=0, keepdims=True).astype(jnp.int32)
    place = (rank // sub) * part + owner.astype(jnp.int32) * sub + rank % sub
    slots = halves * part
    placing_t[...] = (
        (lax.broadcasted_iota(jnp.int32, (slots, rows), 0) == place).astype(F32).astype(BF16)
    )
    place_c = column(place.astype(F32)).astype(jnp.int32)
    lane = lax.broadcasted_iota(jnp.int32, (rows, LANES), 1)
    for t in range(slots // LANES):
        here = (lane + t * LANES == place_c).astype(F32).astype(BF16)
        placing[:, t * LANES : (t + 1) * LANES] = here
    chosen = (lane == column(local_slot).astype(jnp.int32)).astype(F32).astype(BF16)
    lengths[...] = column(fill[...].astype(F32)).astype(jnp.int32)

    loads[0].wait()
    for load in loads[1:4]:
        load.start()
    tile = 512
    for h in range(halves):
        pick = slice(h * part, (h + 1) * part)

        @pl.loop(0, half // tile)
        def _(t):
            cols = pl.ds(pl.multiple_of(t * tile, tile), tile)
            packed = dot(placing_t[pick], hid_v[:, cols]).astype(BF16)
            x_send[h, :, :, cols] = packed.reshape(n, sub, tile)

        packed_chosen = dot(placing_t[pick], chosen).astype(BF16)
        x_send[h, :, :, half:] = packed_chosen.reshape(n, sub, LANES)
        if h == 0:
            pl.semaphore_wait(barrier, n)
        exchange(*hidden_move(h))
    for load in loads[4:]:
        load.start()

    high = scales[...].astype(BF16)
    rest = scales[...] - high.astype(F32)
    middle = rest.astype(BF16)
    low = (rest - middle.astype(F32)).astype(BF16)
    blocks = scales.shape[1]
    block_of = lax.broadcasted_iota(jnp.int32, (blocks, tile), 0)
    block_at = lax.broadcasted_iota(jnp.int32, (blocks, tile), 1) // BLOCK
    for t in range(wide_scales.shape[1] // tile):
        chosen_block = (block_of == block_at + t * (tile // BLOCK)).astype(F32).astype(BF16)
        wide_scales[:, t * tile : (t + 1) * tile] = (
            dot(high, chosen_block) + dot(middle, chosen_block) + dot(low, chosen_block)
        )

    loads[1].wait()
    loads[2].wait()

    def sum_cores(index, shrink, mask):
        pieces = shrink.shape[1] // LANES
        shrink = shrink * mask
        folded = shrink[:, :LANES]
        for t in range(1, pieces):
            folded = folded + shrink[:, t * LANES : (t + 1) * LANES]
        sum_send[index] = folded
        swap = sibling(index, sum_send.at[index], sum_recv.at[index])
        swap.start()
        swap.wait()
        total = (sum_send[index] + sum_recv[index]).astype(BF16).astype(F32)
        return (jnp.concatenate([total] * pieces, axis=1) * mask).astype(BF16)

    def picked(h):
        return x_recv[h, :, :, half:].reshape(part, LANES)

    rank_of = lax.broadcasted_iota(jnp.int32, (part, spread2), 1) % (2 * ADAPTER_RANK)
    is_query = (rank_of < ADAPTER_RANK).astype(F32).astype(BF16)

    def correct(g, h):
        mixed = mixed_v[h]
        mixed_q = mixed * is_query
        table = up_v[:, :, g * group : (g + 1) * group].reshape(spread2, group)
        i = g * halves + h
        corr = (adapter_scale * dot(mixed_q, table)).astype(BF16)
        c_send[i, :, :, :group] = corr.reshape(n, sub, group)
        corr = (adapter_scale * dot(mixed - mixed_q, table)).astype(BF16)
        c_send[i, :, :, group:] = corr.reshape(n, sub, group)
        exchange(*corr_move(g, h))

    for h in range(halves):
        arrived(*hidden_move(h))
        mask = dot(picked(h), indicator((LANES, spread2), 0, 2 * ADAPTER_RANK))
        shrink = dot_t(
            x_recv[h, :, :, :half].reshape(part, half), down_v[...].reshape(spread2, half)
        )
        mixed_v[h] = sum_cores(h, shrink, mask)
        for g in range(GROUPS):
            correct(g, h)

    for index in range(3, 9):
        loads[index].wait()
    inverse_root = 1.0 / math.sqrt(HEAD_DIM)
    cache = keys_v.shape[1]
    gather = indicator((group, LANES), 1, HEAD_DIM)
    spreadm = indicator((LANES, group), 0, HEAD_DIM)
    position = lax.broadcasted_iota(jnp.int32, (ROW_BLOCK, cache, LANES), 1)
    for g in range(GROUPS):
        cols = slice(g * group, (g + 1) * group)
        corr = None
        for h in range(halves):
            arrived(*corr_move(g, h))
            term = dot(
                placing[:, h * part : (h + 1) * part],
                c_recv[g * halves + h].reshape(part, 2 * group),
            )
            corr = term if corr is None else corr + term
        q_v[:, cols] = (bq_v[:, cols].astype(F32) + corr[:, :group]).astype(BF16)
        vnew_v[:, cols] = (bv_v[:, cols].astype(F32) + corr[:, group:]).astype(BF16)

        @pl.loop(0, rows // ROW_BLOCK)
        def _(i):
            block = pl.ds(pl.multiple_of(i * ROW_BLOCK, ROW_BLOCK), ROW_BLOCK)
            q = q_v[block, cols].astype(F32)
            product = keys_v[block, :, cols].astype(F32) * q[:, None, :]
            score = dot_split(product.reshape(ROW_BLOCK * cache, group), gather) * inverse_root
            score = score.reshape(ROW_BLOCK, cache, LANES)
            own = dot_split(q * kin_v[block, cols].astype(F32), gather) * inverse_root
            usable = position < lengths[block, :][:, None, :]
            score = jnp.where(usable, score, -jnp.inf)
            highest = jnp.maximum(jnp.max(score, axis=1), own)
            e = jnp.exp(score - highest[:, None, :])
            own_e = jnp.exp(own - highest)
            denominator = jnp.sum(e, axis=1) + own_e
            w = (e / denominator[:, None, :]).reshape(ROW_BLOCK * cache, LANES).astype(BF16)
            own_w = (own_e / denominator).astype(BF16)
            wide = dot(w, spreadm).reshape(ROW_BLOCK, cache, group)
            context = jnp.sum(wide * vals_v[block, :, cols].astype(F32), axis=1)
            context = context + dot(own_w, spreadm) * vnew_v[block, cols].astype(F32)
            ctx_v[block, cols] = context.astype(BF16)

        for h in range(halves):
            packed = dot(placing_t[h * part : (h + 1) * part], ctx_v[:, cols]).astype(BF16)
            t_send[g * halves + h] = packed.reshape(n, sub, group)
            exchange(*context_move(g, h))

    loads[9].wait()
    loads[10].wait()

    def project(columns):
        total = None
        for k in range(width // BLOCK):
            span = slice(k * BLOCK, (k + 1) * BLOCK)
            term = dot(ctx_v[:, span], w_v[span, columns]) * wide_scales[k : k + 1, columns]
            total = term if total is None else total + term
        return total

    @pl.loop(0, out_half // tile)
    def _(t):
        columns = pl.ds(pl.multiple_of(other * out_half + t * tile, tile), tile)
        base_send[:, pl.ds(pl.multiple_of(t * tile, tile), tile)] = project(columns)

    base_swap = sibling(2 * halves, base_send, base_recv)

    for h in range(halves):
        omask = dot(picked(h), indicator((LANES, orows), 0, ADAPTER_RANK))
        oshrink = None
        for g in range(GROUPS):
            arrived(*context_move(g, h))
            term = dot_t(
                t_recv[g * halves + h].reshape(part, group),
                odown_v[:, :, g * group : (g + 1) * group].reshape(orows, group),
            )
            oshrink = term if oshrink is None else oshrink + term
        omixed_v[h] = sum_cores(halves + h, oshrink, omask)
        for c in range(OUT_CHUNKS):
            table = oup_v[:, :, c * out_chunk : (c + 1) * out_chunk].reshape(orows, out_chunk)
            corr = (adapter_scale * dot(omixed_v[h], table)).astype(BF16)
            o_send[h * OUT_CHUNKS + c] = corr.reshape(n, sub, out_chunk)
            exchange(*out_move(h, c))
    base_swap.start()

    @pl.loop(0, out_half // tile)
    def _(t):
        columns = pl.ds(pl.multiple_of(tp * out_half + t * tile, tile), tile)
        base_own[:, pl.ds(pl.multiple_of(t * tile, tile), tile)] = project(columns)

    base_swap.wait()
    for h in range(halves):
        for c in range(OUT_CHUNKS):
            cols = slice(c * out_chunk, (c + 1) * out_chunk)
            arrived(*out_move(h, c))
            total = base_own[:, cols] + dot(
                placing[:, h * part : (h + 1) * part],
                o_recv[h * OUT_CHUNKS + c].reshape(part, out_chunk),
            )
            if h == 0:
                total = total + base_recv[:, cols]
            if h == halves - 1:
                out[:, cols] = total.astype(BF16)
            else:
                base_own[:, cols] = total

    for h in range(halves):
        sent(*hidden_move(h))
        for g in range(GROUPS):
            sent(*corr_move(g, h))
            sent(*context_move(g, h))
        for c in range(OUT_CHUNKS):
            sent(*out_move(h, c))


def shards(
    normed_hidden_rows,
    base_query_rows,
    incoming_key,
    base_value_rows,
    stored_keys,
    stored_values,
    cache_fill_length,
    adapter_of_row,
    adapter_pool_row,
    output_projection_weight,
    output_block_scales,
    query_value_down_maps,
    query_value_up_maps,
    output_down_maps,
    output_up_maps,
):
    n = lax.axis_size("req")
    spread = query_value_down_maps.shape[0]
    rows, model_width = normed_hidden_rows.shape
    width = base_query_rows.shape[1]
    halves = (2 * ((rows + n - 1) // n) + SUB - 1) // SUB
    part = n * SUB
    slots = halves * part
    half = model_width // lax.axis_size("tp")
    out_half = output_up_maps.shape[2]
    group = width // GROUPS
    out_chunk = out_half // OUT_CHUNKS
    vmem = pl.BlockSpec(memory_space=pltpu.VMEM)
    hbm = pl.BlockSpec(memory_space=pl.ANY)

    def like(x):
        return pltpu.VMEM(x.shape, x.dtype)

    dma = pltpu.SemaphoreType.DMA
    return pl.pallas_call(
        kernel,
        out_shape=jax.ShapeDtypeStruct((rows, out_half), BF16),
        in_specs=[vmem] * 4 + [hbm] * 11,
        out_specs=vmem,
        scratch_shapes=[
            pltpu.VMEM((rows, half), BF16),
            like(base_query_rows),
            like(incoming_key),
            like(base_value_rows),
            like(stored_keys),
            like(stored_values),
            like(output_projection_weight),
            pltpu.VMEM((spread, query_value_down_maps.shape[1], half), BF16),
            like(query_value_up_maps),
            like(output_down_maps),
            like(output_up_maps),
            pltpu.VMEM((rows, slots), BF16),
            pltpu.VMEM((slots, rows), BF16),
            pltpu.VMEM((rows, LANES), jnp.int32),
            pltpu.VMEM((output_block_scales.shape[0], model_width), F32),
            pltpu.VMEM((halves, n, SUB, half + LANES), BF16),
            pltpu.VMEM((halves, n, SUB, half + LANES), BF16),
            pltpu.VMEM((GROUPS * halves, n, SUB, 2 * group), BF16),
            pltpu.VMEM((GROUPS * halves, n, SUB, 2 * group), BF16),
            pltpu.VMEM((GROUPS * halves, n, SUB, group), BF16),
            pltpu.VMEM((GROUPS * halves, n, SUB, group), BF16),
            pltpu.VMEM((OUT_CHUNKS * halves, n, SUB, out_chunk), BF16),
            pltpu.VMEM((OUT_CHUNKS * halves, n, SUB, out_chunk), BF16),
            pltpu.VMEM((2 * halves, part, LANES), F32),
            pltpu.VMEM((2 * halves, part, LANES), F32),
            pltpu.VMEM((rows, out_half), F32),
            pltpu.VMEM((rows, out_half), F32),
            pltpu.VMEM((rows, out_half), F32),
            pltpu.VMEM((rows, width), BF16),
            pltpu.VMEM((rows, width), BF16),
            pltpu.VMEM((rows, width), BF16),
            pltpu.VMEM((halves, part, spread * 2 * ADAPTER_RANK), BF16),
            pltpu.VMEM((halves, part, spread * ADAPTER_RANK), BF16),
            dma((11,)),
            dma((halves, n)),
            dma((halves, n)),
            dma((GROUPS * halves, n)),
            dma((GROUPS * halves, n)),
            dma((GROUPS * halves, n)),
            dma((GROUPS * halves, n)),
            dma((OUT_CHUNKS * halves, n)),
            dma((OUT_CHUNKS * halves, n)),
            dma((2 * halves + 1,)),
            dma((2 * halves + 1,)),
        ],
        compiler_params=pltpu.CompilerParams(
            collective_id=0, has_side_effects=True, vmem_limit_bytes=58 * 1024 * 1024
        ),
    )(
        adapter_of_row[None, :], adapter_pool_row[None, :], cache_fill_length[None, :],
        output_block_scales, normed_hidden_rows, base_query_rows, incoming_key, base_value_rows,
        stored_keys, stored_values, output_projection_weight,
        query_value_down_maps, query_value_up_maps, output_down_maps, output_up_maps,
    )


def solution(mesh):
    in_specs = (
        P(("replica", "req"), None),
        P(("replica", "req"), "tp"),
        P(("replica", "req"), "tp"),
        P(("replica", "req"), "tp"),
        P(("replica", "req"), None, "tp"),
        P(("replica", "req"), None, "tp"),
        P(("replica", "req")),
        P(("replica", "req")),
        P("replica"),
        P("tp", None),
        P("tp", None),
        P("req", None, None),
        P("req", None, "tp"),
        P("req", None, "tp"),
        P("req", None, "tp"),
    )
    out_specs = P(("replica", "req"), "tp")
    return jax.shard_map(shards, mesh=mesh, in_specs=in_specs, out_specs=out_specs, check_vma=False)
```
